512 devices in a mesh: rep: 16 (over z_hi, x, core), fsdp: 32 (over z_lo, y).
Axes of the slice: x: 4, y: 4, z: 16 (z_hi: 2, z_lo: 8; z = z_hi * 8 + z_lo), core: 2. Of those that a mesh axis runs over, the one named last changes fastest.
Arguments:
- hidden_in: bfloat16 [65536, 8192], P(('rep', 'fsdp')), may hold values from -6 to 6
- gain: float32 [8192], replicated, may hold values from 0.5 to 1.5
- key_grad: bfloat16 [65536, 512], P(('rep', 'fsdp')), may hold values from -6 to 6
- weights: float32 [16, 8192, 512], P('rep', 'fsdp'), may hold values from -6 to 6
- first_moment: float32 [16, 8192, 512], P('rep', 'fsdp'), may hold values from -1 to 1
- second_moment: bfloat16 [16, 8192, 512], P('rep', 'fsdp'), may hold values from 0.0099487305 to 0.099609375
- anchor: float32 [8192, 256], P('fsdp'), may hold values from -6 to 6
- momentum: float32 [8192, 256], P('fsdp'), may hold values from -4 to 4
- fragment: int32 [1], replicated, may hold values from 0 to 1
Outputs:
- keys: bfloat16 [65536, 512], P(('rep', 'fsdp'))
- weights_out: float32 [16, 8192, 512], P('rep', 'fsdp')
- momentum_out: float32 [8192, 256], P('fsdp')
The draws below stay inside these ranges and needn't reach their ends.
All inputs are finite; a program needn't handle non-finite values.
Results may differ from the reference program's by a relative error of at most 0.012.
Values may be sent and summed in bfloat16 or wider, within the bound.
No kernel may reach another device: no remote copies, remote signals or barrier semaphores. Data moves between devices by JAX's collectives and lax.ppermute only.
A program may use at most 64 MiB of HBM per device.

```python
import math
import jax
import jax.numpy as jnp
from jax import lax

D = 8192
NFRAG = 2
TOK_DEV = 128
KW = 512
FW = 256
TOKENS = 65536
N_REP = 16
N_FSDP = 32


def steps_of(own_key, dims, split, smallest, high):
    def one(dim, parts):
        steps = jax.random.uniform(jax.random.fold_in(jax.random.fold_in(own_key, 6), dim), (parts,), jnp.float32, smallest / len(split), high / len(split))
        return jnp.repeat(jnp.exp(steps), dims[dim] // parts).reshape((-1,) + (1,) * (len(dims) - dim - 1))

    factor_of = one(*split[0])
    for cut in split[1:]:
        factor_of = factor_of * one(*cut)
    return factor_of


def gaussian(rng, shape, spread, most, split=(), kind=jnp.bfloat16):
    array = spread * jax.random.normal(rng, shape, jnp.float32)
    if split:
        array = array * steps_of(rng, shape, split, -0.22, 0.18)
    return jnp.clip(array, -most, most).astype(kind)


def setup_inputs(seed: int = 0) -> dict:
    splits = jax.random.split(jax.random.key(seed), 10)
    return {
        "hidden_in": gaussian(splits[0], (TOKENS, D), 1.0, 6.0, ((0, 512),)),
        "gain": jnp.clip(1.0 + 0.1 * jax.random.normal(splits[1], (D,), jnp.float32), 0.5, 1.5),
        "key_grad": gaussian(splits[2], (TOKENS, KW), 1.0, 6.0, ((0, 512),)),
        "weights": gaussian(splits[3], (N_REP, D, KW), 1.0, 6.0, ((0, 16), (1, 32)), jnp.float32),
        "first_moment": gaussian(splits[4], (N_REP, D, KW), 0.2, 1.0, ((0, 16), (1, 32)), jnp.float32),
        "second_moment": jnp.clip(jnp.exp(math.log(0.099609375) - 2.3038113 * jax.random.uniform(splits[5], (N_REP, D, KW), jnp.float32) ** steps_of(splits[5], (N_REP, D, KW), ((0, 16), (1, 32)), -0.2, 0.2)), 0.0099487305, 0.099609375).astype(jnp.bfloat16),
        "anchor": gaussian(splits[6], (D, FW), 1.0, 6.0, ((0, 32),), jnp.float32),
        "momentum": gaussian(splits[7], (D, FW), 0.5, 4.0, ((0, 32),), jnp.float32),
        "fragment": jax.random.randint(splits[8], (1,), 0, NFRAG).astype(jnp.int32),
    }


NORM_EPS = 1e-05
ADAM_EPS = 1e-08
INNER_RATE = 0.6

def outer_step(mean_cols, anchor_part, momentum_part):
    delta = anchor_part - mean_cols
    momentum_next = 0.9 * momentum_part + delta
    return (anchor_part - 0.7 * (delta + 0.9 * momentum_next), momentum_next)

def reference(hidden_in, gain, key_grad, weights, first_moment, second_moment, anchor, momentum, fragment):
    multiplier = float(D) ** (-0.5)
    block_rows = D // N_FSDP
    inputs = hidden_in.reshape(N_REP, N_FSDP * TOK_DEV, D)
    cotangent = key_grad.reshape(N_REP, N_FSDP * TOK_DEV, KW)

    def per_replica(packed):
        tokens_in, grads_in, weight_now, moment_one, moment_two = packed
        tokens_f = tokens_in.astype(jnp.float32)
        factor = lax.rsqrt(lax.optimization_barrier(jnp.mean(tokens_f * tokens_f, axis=1, keepdims=True)) + NORM_EPS)
        normed = (tokens_f * factor * gain).astype(jnp.bfloat16)
        weight_low = weight_now.astype(jnp.bfloat16)

        def add_block(summed, block_index):
            offset = (block_index * block_rows).astype(jnp.int32)
            left = lax.dynamic_slice_in_dim(normed, offset, block_rows, 1)
            right = lax.dynamic_slice_in_dim(weight_low, offset, block_rows, 0)
            partial_value = jnp.dot(left, right, preferred_element_type=jnp.float32) * multiplier
            rounded = lax.optimization_barrier(partial_value.astype(jnp.bfloat16))
            return (summed + rounded.astype(jnp.float32), None)
        summed, unused = lax.scan(add_block, jnp.zeros((N_FSDP * TOK_DEV, KW), jnp.float32), jnp.arange(N_FSDP, dtype=jnp.int32))
        keys = summed.astype(jnp.bfloat16)
        gradient = jnp.dot(normed.T, grads_in, preferred_element_type=jnp.float32) * multiplier
        moment_next = 0.9 * moment_one + 0.1 * gradient
        second_next = 0.95 * moment_two.astype(jnp.float32) + 0.05 * gradient * gradient
        inner = weight_now - INNER_RATE * (moment_next / (jnp.sqrt(second_next) + ADAM_EPS) + 0.1 * weight_now)
        return (keys, inner)
    keys, inner = lax.map(per_replica, (inputs, cotangent, weights, first_moment, second_moment))
    frag_width = anchor.shape[1]
    col_offset = (fragment[0] * frag_width).astype(jnp.int32)
    start_cols = lax.dynamic_slice_in_dim(weights, col_offset, frag_width, 2)
    mean_cols = lax.optimization_barrier(jnp.sum(start_cols, axis=0)) / N_REP
    fresh, momentum_out = outer_step(mean_cols, anchor, momentum)
    current = lax.dynamic_slice_in_dim(inner, col_offset, frag_width, 2)
    merged = 0.5 * current + 0.5 * fresh[None]
    weights_out = lax.dynamic_update_slice_in_dim(inner, merged, col_offset, 2)
    return (keys.reshape(N_REP * N_FSDP * TOK_DEV, KW), weights_out, momentum_out)
```

```python
import jax
import jax.numpy as jnp
from jax import lax
from jax.experimental import pallas as pl
from jax.experimental.pallas import tpu as pltpu
from jax.sharding import Mesh, PartitionSpec as P

NORM_EPS = 1e-05
ADAM_EPS = 1e-08
INNER_RATE = 0.6

REP = ("zh", "x", "c")
FSDP = ("zq", "zp", "y")
NEAR = ("zp", "y")
VMEM = pl.BlockSpec(memory_space=pltpu.VMEM)
SMEM = pl.BlockSpec(memory_space=pltpu.SMEM)
PARAMS = pltpu.CompilerParams(vmem_limit_bytes=32 * 1024 * 1024)


def outer_step(mean_cols, anchor_part, momentum_part):
    delta = anchor_part - mean_cols
    momentum_next = 0.9 * momentum_part + delta
    return (anchor_part - 0.7 * (delta + 0.9 * momentum_next), momentum_next)


def swap(value, bit):
    return lax.ppermute(value, "zq", [(i, i ^ bit) for i in range(4)])


def flip(value, axis, bit=1):
    return lax.ppermute(value, axis, [(i, i ^ bit) for i in range(lax.axis_size(axis))])


def add(a, b):
    return (a.astype(jnp.float32) + b.astype(jnp.float32)).astype(jnp.bfloat16)


def after(value, *others):
    return lax.optimization_barrier((value, *others))[0]


def exchange(value, axes):
    return lax.all_to_all(value, axes, split_axis=0, concat_axis=0, tiled=True)


def kernel_call(body, outs, args, flops=0, scalars=0, scratch=()):
    moved = sum(a.size * a.dtype.itemsize for a in (*args, *outs))
    return pl.pallas_call(
        body,
        out_shape=outs,
        in_specs=[SMEM] * scalars + [VMEM] * (len(args) - scalars),
        out_specs=[VMEM] * len(outs),
        scratch_shapes=list(scratch),
        compiler_params=PARAMS,
        cost_estimate=pl.CostEstimate(flops=flops, bytes_accessed=moved, transcendentals=0),
    )(*args)


def pack_tiles(far, near, rows, hidden_ref, tiles_ref):
    for a in range(near):
        for q in range(far):
            tiles_ref[a, :, q * rows : (q + 1) * rows] = hidden_ref[:, (q * near + a) * rows : (q * near + a + 1) * rows]


def scale_tokens(hidden_ref, grad_ref, factor_ref, scaled_ref):
    tokens, features = hidden_ref.shape
    wide = 512
    total = jnp.zeros((tokens, wide), jnp.float32)
    for i in range(features // wide):
        part = hidden_ref[:, i * wide : (i + 1) * wide].astype(jnp.float32)
        total = total + part * part
    mean = jnp.sum(total, axis=1, keepdims=True) / features
    factor = lax.rsqrt(mean + NORM_EPS)
    factor_ref[...] = factor
    scaled_ref[...] = (grad_ref[...].astype(jnp.float32) * factor).astype(jnp.bfloat16)


def block_of(place_ref, dh, dl, rows):
    block = (place_ref[0] ^ dh) * 2 + (place_ref[1] ^ dl)
    return pl.ds(pl.multiple_of(block * rows, rows), rows)


def gradient_blocks(rows, tokens, place_ref, tiles_ref, g0, g1, g2, g3, keep_a, keep_b, send_a, send_b, grad_ref):
    half = grad_ref.shape[1] // 2
    for turn, piece in enumerate((g0, g1, g2, g3)):
        for j in range(2):
            source = (place_ref[2] ^ j) * 4 + ((place_ref[3] + 4 - turn) & 3)
            where = pl.ds(pl.multiple_of(source * tokens, tokens), tokens)
            grad_ref[where, :] = piece[j * tokens : (j + 1) * tokens, :]
    for dh in range(2):
        for dl in range(2):
            left = tiles_ref[:, block_of(place_ref, dh, dl, rows)]
            value = lax.dot_general(left, grad_ref[...], (((0,), (0,)), ((), ())), preferred_element_type=jnp.float32)
            if dl:
                send_a[dh] = value[:, :half].astype(jnp.bfloat16)
            else:
                keep_a[dh] = value[:, :half]
            if dh:
                send_b[dl] = value[:, half:].astype(jnp.bfloat16)
            else:
                keep_b[dl] = value[:, half:]


def key_partials(rows, multiplier, place_ref, tiles_ref, pair_ref, other_ref, out_ref):
    total = None
    for dh in range(2):
        for dl in range(2):
            left = tiles_ref[:, block_of(place_ref, dh, dl, rows)]
            right = (other_ref if dl else pair_ref)[dh]
            value = jnp.dot(left, right, preferred_element_type=jnp.float32)
            total = value if total is None else total + value
    out_ref[...] = (total * multiplier).astype(jnp.bfloat16)


def on_device(
    hidden_in, gain, key_grad, weights, first_moment, second_moment, anchor, momentum, fragment
):
    tokens, features = hidden_in.shape
    key_width = key_grad.shape[1]
    half = key_width // 2
    multiplier = float(features) ** (-0.5)
    weight_now = weights[0]
    rows = weight_now.shape[0]
    near = lax.axis_size(NEAR)
    far = lax.axis_size("zq")
    far_index = lax.axis_index("zq")
    place = jnp.stack([far_index >> 1, far_index & 1, lax.axis_index("zp"), lax.axis_index("y")]).astype(jnp.int32)
    shape = jax.ShapeDtypeStruct
    f32, b16 = jnp.float32, jnp.bfloat16

    (tiles,) = kernel_call(
        lambda *refs: pack_tiles(far, near, rows, *refs), [shape((near, tokens, far * rows), b16)], (hidden_in,)
    )
    tiles = exchange(tiles, NEAR).reshape(near * tokens, far * rows)

    own_gain = lax.dynamic_slice_in_dim(gain, lax.axis_index(FSDP) * rows, rows, 0)[:, None]
    weight_low = (weight_now * own_gain).astype(b16)
    pair = jnp.stack([weight_low, swap(weight_low, 2)])
    other_pair = swap(pair, 1)

    factor, scaled_grad = kernel_call(
        scale_tokens, [shape((tokens, 1), f32), shape((tokens, key_width), b16)], (hidden_in, key_grad)
    )
    both_grad = jnp.concatenate([scaled_grad, flip(scaled_grad, "zp")])
    turned = [lax.ppermute(both_grad, "y", [(i, (i + k) % 4) for i in range(4)]) for k in (1, 3, 2)]
    grads = (both_grad, turned[0], turned[2], turned[1])

    frag_width = anchor.shape[1]
    col_offset = fragment[0] * frag_width
    start_cols = lax.dynamic_slice_in_dim(weight_now, col_offset, frag_width, 1).astype(b16)
    core = lax.axis_index("c")
    mine = lax.dynamic_slice_in_dim(start_cols, core * (rows // 2), rows // 2, 0)
    theirs = lax.dynamic_slice_in_dim(start_cols, (1 - core) * (rows // 2), rows // 2, 0)
    part = add(mine, flip(theirs, "c"))

    flops = 2 * near * tokens * far * rows * key_width
    block = (2, rows, half)
    keep_a, keep_b, send_a, send_b = kernel_call(
        lambda *refs: gradient_blocks(rows, tokens, *refs),
        [shape(block, f32), shape(block, f32), shape(block, b16), shape(block, b16)],
        (place, after(tiles, pair, part, *grads), *grads),
        flops,
        1,
        [pltpu.VMEM((near * tokens, key_width), b16)],
    )
    sum_a = keep_a + swap(send_a, 1).astype(f32)
    sum_b = keep_b + swap(send_b, 2).astype(f32)
    part = add(part, flip(part, "x", 1))
    part = add(part, flip(part, "x", 2))

    (partial_keys,) = kernel_call(
        lambda *refs: key_partials(rows, multiplier, *refs),
        [shape((near * tokens, key_width), b16)],
        (place, tiles, pair, other_pair),
        flops,
        1,
    )
    rest_a, rest_b = sum_a[1].astype(b16), sum_b[1].astype(b16)
    rest_a, rest_b, partial_keys, part = lax.optimization_barrier((rest_a, rest_b, partial_keys, part))
    grad_a = sum_a[0] + swap(rest_a, 2).astype(f32)
    grad_b = sum_b[0] + swap(rest_b, 1).astype(f32)
    grad_sum = jnp.concatenate([grad_a, grad_b], axis=1)
    rounded = exchange(partial_keys.reshape(near, tokens, key_width), NEAR)
    keys = (jnp.sum(rounded.astype(f32), axis=0) * factor).astype(b16)

    gradient = grad_sum * (multiplier * own_gain)
    moment_next = 0.9 * first_moment[0] + 0.1 * gradient
    second_next = 0.95 * second_moment[0].astype(f32) + 0.05 * gradient * gradient
    inner = weight_now - INNER_RATE * (
        moment_next / (jnp.sqrt(second_next) + ADAM_EPS) + 0.1 * weight_now
    )
    part = add(part, flip(part, "zh"))
    other = flip(part, "c")
    summed_cols = jnp.where(core == 0, jnp.concatenate([part, other]), jnp.concatenate([other, part])).astype(f32)
    replicas = lax.axis_size(REP)
    fresh, momentum_out = outer_step(summed_cols / replicas, anchor, momentum)
    current = lax.dynamic_slice_in_dim(inner, col_offset, frag_width, 1)
    merged = 0.5 * current + 0.5 * fresh
    weights_out = lax.dynamic_update_slice_in_dim(inner, merged, col_offset, 1)
    return (keys, weights_out[None], momentum_out)


def solution(mesh):
    fine = Mesh(mesh.devices.reshape(2, 4, 2, 4, 2, 4), REP + FSDP)
    both = REP + FSDP
    return jax.shard_map(
        on_device,
        mesh=fine,
        in_specs=(
            P(both, None),
            P(),
            P(both, None),
            P(REP, FSDP, None),
            P(REP, FSDP, None),
            P(REP, FSDP, None),
            P(FSDP, None),
            P(FSDP, None),
            P(),
        ),
        out_specs=(P(both, None), P(REP, FSDP, None), P(FSDP, None)),
        check_vma=False,
    )
```

```python
import jax
import jax.numpy as jnp
from jax import lax
from jax.experimental import pallas as pl
from jax.experimental.pallas import tpu as pltpu
from jax.sharding import Mesh, PartitionSpec as P

NORM_EPS = 1e-05
ADAM_EPS = 1e-08
INNER_RATE = 0.6

REP = ("zh", "x", "c")
FSDP = ("zq", "zp", "y")
NEAR = ("zp", "y")
VMEM = pl.BlockSpec(memory_space=pltpu.VMEM)
SMEM = pl.BlockSpec(memory_space=pltpu.SMEM)
LAST_COST = 1 << 36
PARAMS = pltpu.CompilerParams(vmem_limit_bytes=8 * 1024 * 1024)


def outer_step(mean_cols, anchor_part, momentum_part):
    delta = anchor_part - mean_cols
    momentum_next = 0.9 * momentum_part + delta
    return (anchor_part - 0.7 * (delta + 0.9 * momentum_next), momentum_next)


def swap(value, bit, name):
    with jax.named_scope(name):
        return lax.ppermute(value, "zq", [(i, i ^ bit) for i in range(4)])


def flip(value, axis, bit=1, name="rep_sum"):
    with jax.named_scope(name):
        return lax.ppermute(value, axis, [(i, i ^ bit) for i in range(lax.axis_size(axis))])


def add(a, b):
    return (a.astype(jnp.float32) + b.astype(jnp.float32)).astype(jnp.bfloat16)


def exchange(value, axes):
    return lax.all_to_all(value, axes, split_axis=0, concat_axis=0, tiled=True)


def kernel_call(body, outs, args, flops=0, scalars=0, scratch=(), behind=()):
    moved = sum(a.size * a.dtype.itemsize for a in (*args, *outs))
    given = len(args)

    def run(*refs):
        body(*refs[:given], *refs[given + len(behind) :])

    args = (*args, *behind)
    return pl.pallas_call(
        run,
        out_shape=outs,
        in_specs=[SMEM] * scalars + [VMEM] * (given - scalars) + [pl.BlockSpec(memory_space=pl.ANY)] * len(behind),
        out_specs=[VMEM] * len(outs),
        scratch_shapes=list(scratch),
        compiler_params=PARAMS,
        cost_estimate=pl.CostEstimate(flops=flops, bytes_accessed=moved, transcendentals=0),
    )(*args)


def prepare(far, near, rows, hidden_ref, grad_ref, tiles_ref, factor_ref):
    tokens, features = hidden_ref.shape
    wide = far * rows
    total = jnp.zeros((tokens, rows), jnp.float32)
    for a in range(near):
        for q in range(far):
            part = hidden_ref[:, (q * near + a) * rows : (q * near + a + 1) * rows]
            tiles_ref[a, :, q * rows : (q + 1) * rows] = part
            part = part.astype(jnp.float32)
            total = total + part * part
    factor = lax.rsqrt(jnp.sum(total, axis=1, keepdims=True) / features + NORM_EPS)
    factor_ref[...] = factor
    scaled = (grad_ref[...].astype(jnp.float32) * factor).astype(jnp.bfloat16)
    for a in range(near):
        tiles_ref[a, :, wide:] = scaled


def block_of(place_ref, dh, dl, rows):
    block = (place_ref[0] ^ dh) * 2 + (place_ref[1] ^ dl)
    return pl.ds(pl.multiple_of(block * rows, rows), rows)


def gradient_blocks(rows, wide, place_ref, tiles_ref, far_ref, part_ref, keep_ref, send_ref, last_ref, part_out):
    for dl in (1, 0):
        for dh in range(2):
            left = tiles_ref[:, block_of(place_ref, dh, dl, rows)]
            value = lax.dot_general(left, tiles_ref[:, wide:], (((0,), (0,)), ((), ())), preferred_element_type=jnp.float32)
            if dl:
                send_ref[dh] = value.astype(jnp.bfloat16)
            else:
                keep_ref[dh] = value
    last_ref[...] = far_ref[...]
    part_out[...] = part_ref[...]


def first_sum(keep_ref, got_ref, mine_ref, send_ref):
    mine_ref[...] = keep_ref[0] + got_ref[0].astype(jnp.float32)
    send_ref[...] = (keep_ref[1] + got_ref[1].astype(jnp.float32)).astype(jnp.bfloat16)


def second_sum(mine_ref, got_ref, grad_ref):
    grad_ref[...] = mine_ref[...] + got_ref[...].astype(jnp.float32)


def key_sum(partial_ref, factor_ref, keys_ref):
    total = partial_ref[0].astype(jnp.float32)
    for i in range(1, partial_ref.shape[0]):
        total = total + partial_ref[i].astype(jnp.float32)
    keys_ref[...] = (total * factor_ref[...]).astype(jnp.bfloat16)


def key_partials(rows, multiplier, place_ref, tiles_ref, *refs):
    total = None
    for dh in range(2):
        for dl in range(2):
            left = tiles_ref[:, block_of(place_ref, dh, dl, rows)]
            right = refs[2 * dh + dl][...]
            value = jnp.dot(left, right, preferred_element_type=jnp.float32)
            total = value if total is None else total + value
    refs[4][...] = (total * multiplier).astype(jnp.bfloat16)


def on_device(
    hidden_in, gain, key_grad, weights, first_moment, second_moment, anchor, momentum, fragment
):
    tokens, features = hidden_in.shape
    key_width = key_grad.shape[1]
    multiplier = float(features) ** (-0.5)
    weight_now = weights[0]
    rows = weight_now.shape[0]
    near = lax.axis_size(NEAR)
    far = lax.axis_size("zq")
    far_index = lax.axis_index("zq")
    place = jnp.stack([far_index >> 1, far_index & 1, lax.axis_index("zp")]).astype(jnp.int32)
    shape = jax.ShapeDtypeStruct
    f32, b16 = jnp.float32, jnp.bfloat16

    wide = far * rows
    tiles, factor = kernel_call(
        lambda *refs: prepare(far, near, rows, *refs),
        [shape((near, tokens, wide + key_width), b16), shape((tokens, 1), f32)],
        (hidden_in, key_grad),
    )
    tiles = exchange(tiles, NEAR).reshape(near * tokens, wide + key_width)

    frag_width = anchor.shape[1]
    col_offset = fragment[0] * frag_width
    start_cols = lax.dynamic_slice_in_dim(weight_now, col_offset, frag_width, 1).astype(b16)
    core = lax.axis_index("c")
    mine = lax.dynamic_slice_in_dim(start_cols, core * (rows // 2), rows // 2, 0)
    theirs = lax.dynamic_slice_in_dim(start_cols, (1 - core) * (rows // 2), rows // 2, 0)
    part = add(mine, flip(theirs, "c"))

    part = add(part, flip(part, "x", 1))

    own_gain = lax.dynamic_slice_in_dim(gain, lax.axis_index(FSDP) * rows, rows, 0)[:, None]
    weight_low = (weight_now * own_gain).astype(b16)
    near_low = swap(weight_low, 1, "weights_near")
    far_low = swap(weight_low, 2, "weights_far")

    flops = 2 * near * tokens * far * rows * key_width
    keep, send, last_low, part = kernel_call(
        lambda *refs: gradient_blocks(rows, wide, *refs),
        [shape((2, rows, key_width), f32), shape((2, rows, key_width), b16), shape(far_low.shape, b16), shape(part.shape, b16)],
        (place, tiles, far_low, part),
        flops,
        1,
        behind=(near_low,),
    )
    got = swap(send, 1, "gradient_near")
    last_low = swap(last_low, 1, "weights_last")
    part = add(part, flip(part, "x", 2))
    part = add(part, flip(part, "zh"))
    other = flip(part, "c")
    summed_cols = jnp.where(core == 0, jnp.concatenate([part, other]), jnp.concatenate([other, part])).astype(f32)
    mine, rest = kernel_call(
        first_sum, [shape((rows, key_width), f32), shape((rows, key_width), b16)], (keep, got)
    )
    last = swap(rest, 2, "gradient_far")
    (grad_sum,) = kernel_call(second_sum, [shape((rows, key_width), f32)], (mine, last), LAST_COST)
    gradient = grad_sum * (multiplier * own_gain)
    moment_next = 0.9 * first_moment[0] + 0.1 * gradient
    second_next = 0.95 * second_moment[0].astype(f32) + 0.05 * gradient * gradient
    inner = weight_now - INNER_RATE * (
        moment_next / (jnp.sqrt(second_next) + ADAM_EPS) + 0.1 * weight_now
    )
    (partial_keys,) = kernel_call(
        lambda *refs: key_partials(rows, multiplier, *refs),
        [shape((near * tokens, key_width), b16)],
        (place, tiles, weight_low, near_low, far_low, last_low),
        flops,
        1,
    )
    partial_keys = exchange(partial_keys.reshape(near, tokens, key_width), NEAR)
    (keys,) = kernel_call(key_sum, [shape((tokens, key_width), b16)], (partial_keys, factor))

    replicas = lax.axis_size(REP)
    fresh, momentum_out = outer_step(summed_cols / replicas, anchor, momentum)
    current = lax.dynamic_slice_in_dim(inner, col_offset, frag_width, 1)
    merged = 0.5 * current + 0.5 * fresh
    weights_out = lax.dynamic_update_slice_in_dim(inner, merged, col_offset, 1)
    return (keys, weights_out[None], momentum_out)


def solution(mesh):
    fine = Mesh(mesh.devices.reshape(2, 4, 2, 4, 2, 4), REP + FSDP)
    both = REP + FSDP
    return jax.shard_map(
        on_device,
        mesh=fine,
        in_specs=(
            P(both, None),
            P(),
            P(both, None),
            P(REP, FSDP, None),
            P(REP, FSDP, None),
            P(REP, FSDP, None),
            P(FSDP, None),
            P(FSDP, None),
            P(),
        ),
        out_specs=(P(both, None), P(REP, FSDP, None), P(FSDP, None)),
        check_vma=False,
    )
```

```python
import jax
import jax.numpy as jnp
from jax import lax
from jax.experimental import pallas as pl
from jax.experimental.pallas import tpu as pltpu
from jax.sharding import Mesh, PartitionSpec as P

NORM_EPS = 1e-05
ADAM_EPS = 1e-08
INNER_RATE = 0.6

REP = ("zh", "x", "c")
FSDP = ("zq", "zp", "y")
NEAR = ("zp", "y")
VMEM = pl.BlockSpec(memory_space=pltpu.VMEM)
SMEM = pl.BlockSpec(memory_space=pltpu.SMEM)
LAST_COST = 1 << 30
KEYS_COST = 1 << 30
RELAY_COST = 1 << 38
PARAMS = pltpu.CompilerParams(vmem_limit_bytes=8 * 1024 * 1024)


def outer_step(mean_cols, anchor_part, momentum_part):
    delta = anchor_part - mean_cols
    momentum_next = 0.9 * momentum_part + delta
    return (anchor_part - 0.7 * (delta + 0.9 * momentum_next), momentum_next)


def swap(value, bit, name):
    with jax.named_scope(name):
        return lax.ppermute(value, "zq", [(i, i ^ bit) for i in range(4)])


def flip(value, axis, bit=1, name="rep_sum"):
    with jax.named_scope(name):
        return lax.ppermute(value, axis, [(i, i ^ bit) for i in range(lax.axis_size(axis))])


def add(a, b):
    return (a.astype(jnp.float32) + b.astype(jnp.float32)).astype(jnp.bfloat16)


def exchange(value, axes):
    return lax.all_to_all(value, axes, split_axis=0, concat_axis=0, tiled=True)


def kernel_call(body, outs, args, flops=0, scalars=0, scratch=(), behind=(), read=0):
    moved = sum(a.size * a.dtype.itemsize for a in (*args, *outs))
    given = len(args)

    def run(*refs):
        body(*refs[: given + read], *refs[given + len(behind) :])

    args = (*args, *behind)
    return pl.pallas_call(
        run,
        out_shape=outs,
        in_specs=[SMEM] * scalars + [VMEM] * (given - scalars) + [pl.BlockSpec(memory_space=pl.ANY)] * len(behind),
        out_specs=[VMEM] * len(outs),
        scratch_shapes=list(scratch),
        compiler_params=PARAMS,
        cost_estimate=pl.CostEstimate(flops=flops, bytes_accessed=moved, transcendentals=0),
    )(*args)


def copy(from_ref, to_ref):
    to_ref[...] = from_ref[...]


def prepare(far, near, rows, hidden_ref, grad_ref, tiles_ref, scaled_ref, factor_ref):
    tokens, features = hidden_ref.shape
    total = jnp.zeros((tokens, rows), jnp.float32)
    for a in range(near):
        for q in range(far):
            part = hidden_ref[:, (q * near + a) * rows : (q * near + a + 1) * rows]
            tiles_ref[a, :, q * rows : (q + 1) * rows] = part
            part = part.astype(jnp.float32)
            total = total + part * part
    factor = lax.rsqrt(jnp.sum(total, axis=1, keepdims=True) / features + NORM_EPS)
    factor_ref[...] = factor
    scaled_ref[...] = (grad_ref[...].astype(jnp.float32) * factor).astype(jnp.bfloat16)


def join_pair(own_ref, other_ref, tiles_ref, both_ref, same_ref):
    tokens = own_ref.shape[0]
    both_ref[:tokens] = own_ref[...]
    both_ref[tokens:] = other_ref[...]


def block_of(place_ref, dh, dl, rows):
    block = (place_ref[0] ^ dh) * 2 + (place_ref[1] ^ dl)
    return pl.ds(pl.multiple_of(block * rows, rows), rows)


def gradient_blocks(rows, place_ref, tiles_ref, part_ref, g0, g1, g2, g3, *refs):
    keep_ref, send_ref, part_out, grad_ref, sems = refs[-5:]
    tokens = g0.shape[0] // 2
    copies = []
    for turn, piece in enumerate((g0, g1, g2, g3)):
        for j in range(2):
            source = (place_ref[2] ^ j) * 4 + ((place_ref[3] + 4 - turn) & 3)
            where = pl.ds(pl.multiple_of(source * tokens, tokens), tokens)
            copies.append(
                pltpu.make_async_copy(piece.at[j * tokens : (j + 1) * tokens], grad_ref.at[where], sems.at[2 * turn + j])
            )
            copies[-1].start()
    part_out[...] = part_ref[...]
    for copy_in in copies:
        copy_in.wait()
    for dl in (1, 0):
        for dh in range(2):
            left = tiles_ref[:, block_of(place_ref, dh, dl, rows)]
            value = lax.dot_general(left, grad_ref[...], (((0,), (0,)), ((), ())), preferred_element_type=jnp.float32)
            if dl:
                send_ref[dh] = value.astype(jnp.bfloat16)
            else:
                keep_ref[dh] = value


def first_sum(keep_ref, got_ref, mine_ref, send_ref):
    mine_ref[...] = keep_ref[0] + got_ref[0].astype(jnp.float32)
    send_ref[...] = (keep_ref[1] + got_ref[1].astype(jnp.float32)).astype(jnp.bfloat16)


def second_sum(mine_ref, got_ref, grad_ref):
    grad_ref[...] = mine_ref[...] + got_ref[...].astype(jnp.float32)


def key_halves(place_ref, partial_ref, mine_ref, send_ref):
    tokens = mine_ref.shape[0]
    for turn, out_ref in ((0, mine_ref), (1, send_ref)):
        where = pl.ds(pl.multiple_of((place_ref[2] ^ turn) * tokens, tokens), tokens)
        total = partial_ref[0, where, :].astype(jnp.float32)
        for y in range(1, partial_ref.shape[0]):
            total = total + partial_ref[y, where, :].astype(jnp.float32)
        out_ref[...] = total.astype(out_ref.dtype)


def key_sum(mine_ref, got_ref, factor_ref, keys_ref):
    keys_ref[...] = ((mine_ref[...] + got_ref[...].astype(jnp.float32)) * factor_ref[...]).astype(jnp.bfloat16)


def key_partials(rows, multiplier, place_ref, tiles_ref, *refs):
    total = None
    for dh in range(2):
        for dl in range(2):
            left = tiles_ref[:, block_of(place_ref, dh, dl, rows)]
            right = refs[2 * dh + dl][...]
            value = jnp.dot(left, right, preferred_element_type=jnp.float32)
            total = value if total is None else total + value
    total = (total * multiplier).astype(jnp.bfloat16)
    out_ref = refs[4]
    tokens = out_ref.shape[1] // 2
    for zp in range(2):
        for y in range(4):
            out_ref[y, zp * tokens : (zp + 1) * tokens, :] = total[(zp * 4 + y) * tokens : (zp * 4 + y + 1) * tokens]


def on_device(
    hidden_in, gain, key_grad, weights, first_moment, second_moment, anchor, momentum, fragment
):
    tokens, features = hidden_in.shape
    key_width = key_grad.shape[1]
    multiplier = float(features) ** (-0.5)
    weight_now = weights[0]
    rows = weight_now.shape[0]
    near = lax.axis_size(NEAR)
    far = lax.axis_size("zq")
    far_index = lax.axis_index("zq")
    place = jnp.stack([far_index >> 1, far_index & 1, lax.axis_index("zp"), lax.axis_index("y")]).astype(jnp.int32)
    shape = jax.ShapeDtypeStruct
    f32, b16 = jnp.float32, jnp.bfloat16

    wide = far * rows
    tiles, scaled, factor = kernel_call(
        lambda *refs: prepare(far, near, rows, *refs),
        [shape((near, tokens, wide), b16), shape(key_grad.shape, b16), shape((tokens, 1), f32)],
        (hidden_in, key_grad),
    )
    other = flip(scaled, "zp", name="cotangent_pair")
    anywhere = pl.BlockSpec(memory_space=pl.ANY)
    both, tiles = pl.pallas_call(
        join_pair,
        out_shape=[shape((2 * tokens, key_width), b16), shape(tiles.shape, b16)],
        in_specs=[VMEM, VMEM, anywhere],
        out_specs=[VMEM, anywhere],
        input_output_aliases={2: 1},
        compiler_params=PARAMS,
    )(scaled, other, tiles)
    tiles = exchange(tiles, NEAR).reshape(near * tokens, wide)
    with jax.named_scope("cotangent_y"):
        turned = [lax.ppermute(both, "y", [(i, (i + k) % 4) for i in range(4)]) for k in (1, 2, 3)]

    frag_width = anchor.shape[1]
    col_offset = fragment[0] * frag_width
    start_cols = lax.dynamic_slice_in_dim(weight_now, col_offset, frag_width, 1).astype(b16)
    core = lax.axis_index("c")
    mine = lax.dynamic_slice_in_dim(start_cols, core * (rows // 2), rows // 2, 0)
    theirs = lax.dynamic_slice_in_dim(start_cols, (1 - core) * (rows // 2), rows // 2, 0)
    part = add(mine, flip(theirs, "c"))

    part = add(part, flip(part, "x", 1))
    part = add(part, flip(part, "x", 2))

    own_gain = lax.dynamic_slice_in_dim(gain, lax.axis_index(FSDP) * rows, rows, 0)[:, None]
    weight_low = (weight_now * own_gain).astype(b16)
    near_low = swap(weight_low, 1, "weights_near")
    far_low = swap(weight_low, 2, "weights_far")
    (relayed,) = kernel_call(copy, [shape(far_low.shape, b16)], (far_low,), RELAY_COST)
    last_low = swap(relayed, 1, "weights_last")

    flops = 2 * near * tokens * far * rows * key_width
    keep, send, part = kernel_call(
        lambda *refs: gradient_blocks(rows, *refs),
        [shape((2, rows, key_width), f32), shape((2, rows, key_width), b16), shape(part.shape, b16)],
        (place, tiles, part),
        flops,
        1,
        [pltpu.VMEM((near * tokens, key_width), b16), pltpu.SemaphoreType.DMA((8,))],
        behind=(both, *turned, near_low, last_low),
        read=4,
    )
    got = swap(send, 1, "gradient_near")
    (partial_keys,) = kernel_call(
        lambda *refs: key_partials(rows, multiplier, *refs),
        [shape((near // 2, 2 * tokens, key_width), b16)],
        (place, tiles, weight_low, near_low, far_low, last_low),
        KEYS_COST,
        1,
        behind=(send,),
    )
    mine, rest = kernel_call(
        first_sum,
        [shape((rows, key_width), f32), shape((rows, key_width), b16)],
        (keep, got),
        behind=(partial_keys,),
    )
    last = swap(rest, 2, "gradient_far")
    part = add(part, flip(part, "zh", name="rep_far"))
    other = flip(part, "c", name="rep_back")
    summed_cols = jnp.where(core == 0, jnp.concatenate([part, other]), jnp.concatenate([other, part])).astype(f32)
    (grad_sum,) = kernel_call(second_sum, [shape((rows, key_width), f32)], (mine, last), LAST_COST)
    gradient = grad_sum * (multiplier * own_gain)
    moment_next = 0.9 * first_moment[0] + 0.1 * gradient
    second_next = 0.95 * second_moment[0].astype(f32) + 0.05 * gradient * gradient
    inner = weight_now - INNER_RATE * (
        moment_next / (jnp.sqrt(second_next) + ADAM_EPS) + 0.1 * weight_now
    )
    partial_keys = exchange(partial_keys, "y")
    own_keys, pair_keys = kernel_call(
        key_halves,
        [shape((tokens, key_width), f32), shape((tokens, key_width), b16)],
        (place, partial_keys),
        scalars=1,
    )
    pair_keys = flip(pair_keys, "zp", name="keys_pair")
    (keys,) = kernel_call(key_sum, [shape((tokens, key_width), b16)], (own_keys, pair_keys, factor))

    replicas = lax.axis_size(REP)
    fresh, momentum_out = outer_step(summed_cols / replicas, anchor, momentum)
    current = lax.dynamic_slice_in_dim(inner, col_offset, frag_width, 1)
    merged = 0.5 * current + 0.5 * fresh
    weights_out = lax.dynamic_update_slice_in_dim(inner, merged, col_offset, 1)
    return (keys, weights_out[None], momentum_out)


def solution(mesh):
    fine = Mesh(mesh.devices.reshape(2, 4, 2, 4, 2, 4), REP + FSDP)
    both = REP + FSDP
    return jax.shard_map(
        on_device,
        mesh=fine,
        in_specs=(
            P(both, None),
            P(),
            P(both, None),
            P(REP, FSDP, None),
            P(REP, FSDP, None),
            P(REP, FSDP, None),
            P(FSDP, None),
            P(FSDP, None),
            P(),
        ),
        out_specs=(P(both, None), P(REP, FSDP, None), P(FSDP, None)),
        check_vma=False,
    )
```

```python
import jax
import jax.numpy as jnp
from jax import lax
from jax.experimental import pallas as pl
from jax.experimental.pallas import tpu as pltpu
from jax.sharding import Mesh, PartitionSpec as P

NORM_EPS = 1e-05
ADAM_EPS = 1e-08
INNER_RATE = 0.6

REP = ("zh", "x", "c")
FSDP = ("zq", "zp", "y")
NEAR = ("zp", "y")
VMEM = pl.BlockSpec(memory_space=pltpu.VMEM)
SMEM = pl.BlockSpec(memory_space=pltpu.SMEM)
LAST_COST = 1 << 30
FIRST_COST = 1 << 34
KEYS_COST = 1 << 30
RELAY_COST = 1 << 38
PARAMS = pltpu.CompilerParams(vmem_limit_bytes=8 * 1024 * 1024)


def outer_step(mean_cols, anchor_part, momentum_part):
    delta = anchor_part - mean_cols
    momentum_next = 0.9 * momentum_part + delta
    return (anchor_part - 0.7 * (delta + 0.9 * momentum_next), momentum_next)


def swap(value, bit, name):
    with jax.named_scope(name):
        return lax.ppermute(value, "zq", [(i, i ^ bit) for i in range(4)])


def flip(value, axis, bit=1, name="rep_sum"):
    with jax.named_scope(name):
        return lax.ppermute(value, axis, [(i, i ^ bit) for i in range(lax.axis_size(axis))])


def add(a, b):
    return (a.astype(jnp.float32) + b.astype(jnp.float32)).astype(jnp.bfloat16)


def exchange(value, axes):
    return lax.all_to_all(value, axes, split_axis=0, concat_axis=0, tiled=True)


def kernel_call(body, outs, args, flops=0, scalars=0, scratch=(), behind=(), read=0):
    moved = sum(a.size * a.dtype.itemsize for a in (*args, *outs))
    given = len(args)

    def run(*refs):
        body(*refs[: given + read], *refs[given + len(behind) :])

    args = (*args, *behind)
    return pl.pallas_call(
        run,
        out_shape=outs,
        in_specs=[SMEM] * scalars + [VMEM] * (given - scalars) + [pl.BlockSpec(memory_space=pl.ANY)] * len(behind),
        out_specs=[VMEM] * len(outs),
        scratch_shapes=list(scratch),
        compiler_params=PARAMS,
        cost_estimate=pl.CostEstimate(flops=flops, bytes_accessed=moved, transcendentals=0),
    )(*args)


def copy(from_ref, to_ref):
    to_ref[...] = from_ref[...]


def prepare(far, near, rows, hidden_ref, grad_ref, tiles_ref, scaled_ref, factor_ref):
    tokens, features = hidden_ref.shape
    total = jnp.zeros((tokens, rows), jnp.float32)
    for a in range(near):
        for q in range(far):
            part = hidden_ref[:, (q * near + a) * rows : (q * near + a + 1) * rows]
            tiles_ref[a, :, q * rows : (q + 1) * rows] = part
            part = part.astype(jnp.float32)
            total = total + part * part
    factor = lax.rsqrt(jnp.sum(total, axis=1, keepdims=True) / features + NORM_EPS)
    factor_ref[...] = factor
    scaled_ref[...] = (grad_ref[...].astype(jnp.float32) * factor).astype(jnp.bfloat16)


def join_pair(own_ref, other_ref, tiles_ref, both_ref, same_ref):
    tokens = own_ref.shape[0]
    both_ref[:tokens] = own_ref[...]
    both_ref[tokens:] = other_ref[...]


def block_of(place_ref, dh, dl, rows):
    block = (place_ref[0] ^ dh) * 2 + (place_ref[1] ^ dl)
    return pl.ds(pl.multiple_of(block * rows, rows), rows)


def gradient_blocks(rows, place_ref, tiles_ref, part_ref, g0, g1, g2, g3, *refs):
    keep_a, keep_b, send_a, send_b, part_out, grad_ref, sems = refs[-7:]
    tokens = g0.shape[0] // 2
    copies = []
    for turn, piece in enumerate((g0, g1, g2, g3)):
        for j in range(2):
            source = (place_ref[2] ^ j) * 4 + ((place_ref[3] + 4 - turn) & 3)
            where = pl.ds(pl.multiple_of(source * tokens, tokens), tokens)
            copies.append(
                pltpu.make_async_copy(piece.at[j * tokens : (j + 1) * tokens], grad_ref.at[where], sems.at[2 * turn + j])
            )
            copies[-1].start()
    part_out[...] = part_ref[...]
    for copy_in in copies:
        copy_in.wait()
    half = keep_a.shape[2]
    for dh in (1, 0):
        for dl in (1, 0):
            left = tiles_ref[:, block_of(place_ref, dh, dl, rows)]
            value = lax.dot_general(left, grad_ref[...], (((0,), (0,)), ((), ())), preferred_element_type=jnp.float32)
            if dl:
                send_a[dh] = value[:, :half].astype(jnp.bfloat16)
            else:
                keep_a[dh] = value[:, :half]
            if dh:
                send_b[dl] = value[:, half:].astype(jnp.bfloat16)
            else:
                keep_b[dl] = value[:, half:]


def first_sum(keep_a, got_a, keep_b, got_b, mine_ref, rest_a, rest_b):
    half = keep_a.shape[2]
    mine_ref[:, :half] = keep_a[0] + got_a[0].astype(jnp.float32)
    mine_ref[:, half:] = keep_b[0] + got_b[0].astype(jnp.float32)
    rest_a[...] = (keep_a[1] + got_a[1].astype(jnp.float32)).astype(jnp.bfloat16)
    rest_b[...] = (keep_b[1] + got_b[1].astype(jnp.float32)).astype(jnp.bfloat16)


def second_sum(mine_ref, got_a, got_b, grad_ref):
    half = got_a.shape[1]
    grad_ref[:, :half] = mine_ref[:, :half] + got_a[...].astype(jnp.float32)
    grad_ref[:, half:] = mine_ref[:, half:] + got_b[...].astype(jnp.float32)


def key_halves(place_ref, partial_ref, mine_ref, send_ref):
    tokens = mine_ref.shape[0]
    for turn, out_ref in ((0, mine_ref), (1, send_ref)):
        where = pl.ds(pl.multiple_of((place_ref[2] ^ turn) * tokens, tokens), tokens)
        total = partial_ref[0, where, :].astype(jnp.float32)
        for y in range(1, partial_ref.shape[0]):
            total = total + partial_ref[y, where, :].astype(jnp.float32)
        out_ref[...] = total.astype(out_ref.dtype)


def key_sum(mine_ref, got_ref, factor_ref, keys_ref):
    keys_ref[...] = ((mine_ref[...] + got_ref[...].astype(jnp.float32)) * factor_ref[...]).astype(jnp.bfloat16)


def key_partials(rows, multiplier, place_ref, tiles_ref, *refs):
    total = None
    for dh in range(2):
        for dl in range(2):
            left = tiles_ref[:, block_of(place_ref, dh, dl, rows)]
            right = refs[2 * dh + dl][...]
            value = jnp.dot(left, right, preferred_element_type=jnp.float32)
            total = value if total is None else total + value
    total = (total * multiplier).astype(jnp.bfloat16)
    out_ref = refs[4]
    tokens = out_ref.shape[1] // 2
    for zp in range(2):
        for y in range(4):
            out_ref[y, zp * tokens : (zp + 1) * tokens, :] = total[(zp * 4 + y) * tokens : (zp * 4 + y + 1) * tokens]


def on_device(
    hidden_in, gain, key_grad, weights, first_moment, second_moment, anchor, momentum, fragment
):
    tokens, features = hidden_in.shape
    key_width = key_grad.shape[1]
    multiplier = float(features) ** (-0.5)
    weight_now = weights[0]
    rows = weight_now.shape[0]
    near = lax.axis_size(NEAR)
    far = lax.axis_size("zq")
    far_index = lax.axis_index("zq")
    place = jnp.stack([far_index >> 1, far_index & 1, lax.axis_index("zp"), lax.axis_index("y")]).astype(jnp.int32)
    shape = jax.ShapeDtypeStruct
    f32, b16 = jnp.float32, jnp.bfloat16

    wide = far * rows
    tiles, scaled, factor = kernel_call(
        lambda *refs: prepare(far, near, rows, *refs),
        [shape((near, tokens, wide), b16), shape(key_grad.shape, b16), shape((tokens, 1), f32)],
        (hidden_in, key_grad),
    )
    other = flip(scaled, "zp", name="cotangent_pair")
    anywhere = pl.BlockSpec(memory_space=pl.ANY)
    both, tiles = pl.pallas_call(
        join_pair,
        out_shape=[shape((2 * tokens, key_width), b16), shape(tiles.shape, b16)],
        in_specs=[VMEM, VMEM, anywhere],
        out_specs=[VMEM, anywhere],
        input_output_aliases={2: 1},
        compiler_params=PARAMS,
    )(scaled, other, tiles)
    tiles = exchange(tiles, NEAR).reshape(near * tokens, wide)
    with jax.named_scope("cotangent_y"):
        turned = [lax.ppermute(both, "y", [(i, (i + k) % 4) for i in range(4)]) for k in (1, 2, 3)]

    frag_width = anchor.shape[1]
    col_offset = fragment[0] * frag_width
    start_cols = lax.dynamic_slice_in_dim(weight_now, col_offset, frag_width, 1).astype(b16)
    core = lax.axis_index("c")
    mine = lax.dynamic_slice_in_dim(start_cols, core * (rows // 2), rows // 2, 0)
    theirs = lax.dynamic_slice_in_dim(start_cols, (1 - core) * (rows // 2), rows // 2, 0)
    part = add(mine, flip(theirs, "c"))

    part = add(part, flip(part, "x", 1))
    part = add(part, flip(part, "x", 2))

    own_gain = lax.dynamic_slice_in_dim(gain, lax.axis_index(FSDP) * rows, rows, 0)[:, None]
    weight_low = (weight_now * own_gain).astype(b16)
    near_low = swap(weight_low, 1, "weights_near")
    far_low = swap(weight_low, 2, "weights_far")
    (relayed,) = kernel_call(copy, [shape(far_low.shape, b16)], (far_low,), RELAY_COST)
    last_low = swap(relayed, 1, "weights_last")

    flops = 2 * near * tokens * far * rows * key_width
    half = key_width // 2
    block = (2, rows, half)
    keep_a, keep_b, send_a, send_b, part = kernel_call(
        lambda *refs: gradient_blocks(rows, *refs),
        [*(shape(block, f32),) * 2, *(shape(block, b16),) * 2, shape(part.shape, b16)],
        (place, tiles, part),
        flops,
        1,
        [pltpu.VMEM((near * tokens, key_width), b16), pltpu.SemaphoreType.DMA((8,))],
        behind=(both, *turned, near_low, last_low),
        read=4,
    )
    got_a, got_b = swap(send_a, 1, "gradient_near"), swap(send_b, 2, "gradient_far")
    (partial_keys,) = kernel_call(
        lambda *refs: key_partials(rows, multiplier, *refs),
        [shape((near // 2, 2 * tokens, key_width), b16)],
        (place, tiles, weight_low, near_low, far_low, last_low),
        KEYS_COST,
        1,
        behind=(send_a,),
    )
    mine, rest_a, rest_b = kernel_call(
        first_sum,
        [shape((rows, key_width), f32), shape((rows, half), b16), shape((rows, half), b16)],
        (keep_a, got_a, keep_b, got_b),
        FIRST_COST,
        behind=(partial_keys,),
    )
    last_a, last_b = swap(rest_a, 2, "gradient_far"), swap(rest_b, 1, "gradient_near")
    part = add(part, flip(part, "zh", name="rep_far"))
    other = flip(part, "c", name="rep_back")
    summed_cols = jnp.where(core == 0, jnp.concatenate([part, other]), jnp.concatenate([other, part])).astype(f32)
    partial_keys = exchange(partial_keys, "y")
    own_keys, pair_keys = kernel_call(
        key_halves,
        [shape((tokens, key_width), f32), shape((tokens, key_width), b16)],
        (place, partial_keys),
        scalars=1,
    )
    pair_keys = flip(pair_keys, "zp", name="keys_pair")
    (grad_sum,) = kernel_call(
        second_sum, [shape((rows, key_width), f32)], (mine, last_a, last_b), LAST_COST, behind=(own_keys,)
    )
    gradient = grad_sum * (multiplier * own_gain)
    moment_next = 0.9 * first_moment[0] + 0.1 * gradient
    second_next = 0.95 * second_moment[0].astype(f32) + 0.05 * gradient * gradient
    inner = weight_now - INNER_RATE * (
        moment_next / (jnp.sqrt(second_next) + ADAM_EPS) + 0.1 * weight_now
    )
    (keys,) = kernel_call(key_sum, [shape((tokens, key_width), b16)], (own_keys, pair_keys, factor))

    replicas = lax.axis_size(REP)
    fresh, momentum_out = outer_step(summed_cols / replicas, anchor, momentum)
    current = lax.dynamic_slice_in_dim(inner, col_offset, frag_width, 1)
    merged = 0.5 * current + 0.5 * fresh
    weights_out = lax.dynamic_update_slice_in_dim(inner, merged, col_offset, 1)
    return (keys, weights_out[None], momentum_out)


def solution(mesh):
    fine = Mesh(mesh.devices.reshape(2, 4, 2, 4, 2, 4), REP + FSDP)
    both = REP + FSDP
    return jax.shard_map(
        on_device,
        mesh=fine,
        in_specs=(
            P(both, None),
            P(),
            P(both, None),
            P(REP, FSDP, None),
            P(REP, FSDP, None),
            P(REP, FSDP, None),
            P(FSDP, None),
            P(FSDP, None),
            P(),
        ),
        out_specs=(P(both, None), P(REP, FSDP, None), P(FSDP, None)),
        check_vma=False,
    )
```

```python
import jax
import jax.numpy as jnp
from jax import lax
from jax.experimental import pallas as pl
from jax.experimental.pallas import tpu as pltpu
from jax.sharding import Mesh, PartitionSpec as P

NORM_EPS = 1e-05
ADAM_EPS = 1e-08
INNER_RATE = 0.6

REP = ("zh", "x", "c")
FSDP = ("zq", "zp", "y")
NEAR = ("zp", "y")
VMEM = pl.BlockSpec(memory_space=pltpu.VMEM)
SMEM = pl.BlockSpec(memory_space=pltpu.SMEM)
LAST_COST = 1 << 30
FIRST_COST = 1 << 34
KEYS_COST = 1 << 30
RELAY_COST = 1 << 38
PARAMS = pltpu.CompilerParams(vmem_limit_bytes=8 * 1024 * 1024)


def outer_step(mean_cols, anchor_part, momentum_part):
    delta = anchor_part - mean_cols
    momentum_next = 0.9 * momentum_part + delta
    return (anchor_part - 0.7 * (delta + 0.9 * momentum_next), momentum_next)


def swap(value, bit, name):
    with jax.named_scope(name):
        return lax.ppermute(value, "zq", [(i, i ^ bit) for i in range(4)])


def flip(value, axis, bit=1, name="rep_sum"):
    with jax.named_scope(name):
        return lax.ppermute(value, axis, [(i, i ^ bit) for i in range(lax.axis_size(axis))])


def add(a, b):
    return (a.astype(jnp.float32) + b.astype(jnp.float32)).astype(jnp.bfloat16)


def exchange(value, axes):
    return lax.all_to_all(value, axes, split_axis=0, concat_axis=0, tiled=True)


def kernel_call(body, outs, args, flops=0, scalars=0, scratch=(), behind=(), read=0):
    moved = sum(a.size * a.dtype.itemsize for a in (*args, *outs))
    given = len(args)

    def run(*refs):
        body(*refs[: given + read], *refs[given + len(behind) :])

    args = (*args, *behind)
    return pl.pallas_call(
        run,
        out_shape=outs,
        in_specs=[SMEM] * scalars + [VMEM] * (given - scalars) + [pl.BlockSpec(memory_space=pl.ANY)] * len(behind),
        out_specs=[VMEM] * len(outs),
        scratch_shapes=list(scratch),
        compiler_params=PARAMS,
        cost_estimate=pl.CostEstimate(flops=flops, bytes_accessed=moved, transcendentals=0),
    )(*args)


def copy(from_ref, to_ref):
    to_ref[...] = from_ref[...]


def prepare(far, near, rows, pick_ref, hidden_ref, grad_ref, now_ref, tiles_ref, scaled_ref, factor_ref, mine_ref, theirs_ref):
    tokens, features = hidden_ref.shape
    count, width = mine_ref.shape
    columns = pl.ds(pl.multiple_of(pick_ref[0] * width, width), width)
    for turn, out_ref in ((0, mine_ref), (1, theirs_ref)):
        part_rows = pl.ds(pl.multiple_of((pick_ref[1] ^ turn) * count, count), count)
        out_ref[...] = now_ref[part_rows, columns].astype(jnp.bfloat16)
    total = jnp.zeros((tokens, rows), jnp.float32)
    for a in range(near):
        for q in range(far):
            part = hidden_ref[:, (q * near + a) * rows : (q * near + a + 1) * rows]
            tiles_ref[a, :, q * rows : (q + 1) * rows] = part
            part = part.astype(jnp.float32)
            total = total + part * part
    factor = lax.rsqrt(jnp.sum(total, axis=1, keepdims=True) / features + NORM_EPS)
    factor_ref[...] = factor
    scaled_ref[...] = (grad_ref[...].astype(jnp.float32) * factor).astype(jnp.bfloat16)


def join_pair(own_ref, other_ref, tiles_ref, both_ref, same_ref):
    tokens = own_ref.shape[0]
    both_ref[:tokens] = own_ref[...]
    both_ref[tokens:] = other_ref[...]


def block_of(place_ref, dh, dl, rows):
    block = (place_ref[0] ^ dh) * 2 + (place_ref[1] ^ dl)
    return pl.ds(pl.multiple_of(block * rows, rows), rows)


def gradient_blocks(rows, place_ref, part_ref, tiles_in, g0, g1, g2, g3, *refs):
    keep_a, keep_b, send_a, send_b, part_out, grad_ref, tiles_ref, sems = refs[-8:]
    tokens = g0.shape[0] // 2
    copies = []
    for turn, piece in enumerate((g0, g1, g2, g3)):
        for j in range(2):
            source = (place_ref[2] ^ j) * 4 + ((place_ref[3] + 4 - turn) & 3)
            where = pl.ds(pl.multiple_of(source * tokens, tokens), tokens)
            copies.append(
                pltpu.make_async_copy(piece.at[j * tokens : (j + 1) * tokens], grad_ref.at[where], sems.at[2 * turn + j])
            )
            copies[-1].start()
    slots = [(1, 1), (1, 0), (0, 1), (0, 0)]
    loads = []
    for k, (dh, dl) in enumerate(slots):
        loads.append(
            pltpu.make_async_copy(
                tiles_in.at[:, block_of(place_ref, dh, dl, rows)],
                tiles_ref.at[:, k * rows : (k + 1) * rows],
                sems.at[8 + k],
            )
        )
        loads[-1].start()
    part_out[...] = part_ref[...]
    for copy_in in copies:
        copy_in.wait()
    half = keep_a.shape[2]
    for dh in (1, 0):
        for dl in (1, 0):
            k = slots.index((dh, dl))
            loads[k].wait()
            left = tiles_ref[:, k * rows : (k + 1) * rows]
            value = lax.dot_general(left, grad_ref[...], (((0,), (0,)), ((), ())), preferred_element_type=jnp.float32)
            if dl:
                send_a[dh] = value[:, :half].astype(jnp.bfloat16)
            else:
                keep_a[dh] = value[:, :half]
            if dh:
                send_b[dl] = value[:, half:].astype(jnp.bfloat16)
            else:
                keep_b[dl] = value[:, half:]


def first_sum(keep_a, got_a, keep_b, got_b, mine_ref, rest_a, rest_b):
    half = keep_a.shape[2]
    mine_ref[:, :half] = keep_a[0] + got_a[0].astype(jnp.float32)
    mine_ref[:, half:] = keep_b[0] + got_b[0].astype(jnp.float32)
    rest_a[...] = (keep_a[1] + got_a[1].astype(jnp.float32)).astype(jnp.bfloat16)
    rest_b[...] = (keep_b[1] + got_b[1].astype(jnp.float32)).astype(jnp.bfloat16)


def second_sum(mine_ref, got_a, got_b, grad_ref):
    half = got_a.shape[1]
    grad_ref[:, :half] = mine_ref[:, :half] + got_a[...].astype(jnp.float32)
    grad_ref[:, half:] = mine_ref[:, half:] + got_b[...].astype(jnp.float32)


def key_halves(place_ref, partial_ref, mine_ref, send_ref):
    tokens = mine_ref.shape[0]
    for turn, out_ref in ((0, mine_ref), (1, send_ref)):
        where = pl.ds(pl.multiple_of((place_ref[2] ^ turn) * tokens, tokens), tokens)
        total = partial_ref[0, where, :].astype(jnp.float32)
        for y in range(1, partial_ref.shape[0]):
            total = total + partial_ref[y, where, :].astype(jnp.float32)
        out_ref[...] = total.astype(out_ref.dtype)


def key_sum(mine_ref, got_ref, factor_ref, keys_ref):
    keys_ref[...] = ((mine_ref[...] + got_ref[...].astype(jnp.float32)) * factor_ref[...]).astype(jnp.bfloat16)


def key_partials(rows, multiplier, place_ref, tiles_ref, *refs):
    total = None
    for dh in range(2):
        for dl in range(2):
            left = tiles_ref[:, block_of(place_ref, dh, dl, rows)]
            right = refs[2 * dh + dl][...]
            value = jnp.dot(left, right, preferred_element_type=jnp.float32)
            total = value if total is None else total + value
    total = (total * multiplier).astype(jnp.bfloat16)
    out_ref = refs[4]
    tokens = out_ref.shape[1] // 2
    for zp in range(2):
        for y in range(4):
            out_ref[y, zp * tokens : (zp + 1) * tokens, :] = total[(zp * 4 + y) * tokens : (zp * 4 + y + 1) * tokens]


def on_device(
    hidden_in, gain, key_grad, weights, first_moment, second_moment, anchor, momentum, fragment
):
    tokens, features = hidden_in.shape
    key_width = key_grad.shape[1]
    multiplier = float(features) ** (-0.5)
    weight_now = weights[0]
    rows = weight_now.shape[0]
    near = lax.axis_size(NEAR)
    far = lax.axis_size("zq")
    far_index = lax.axis_index("zq")
    place = jnp.stack([far_index >> 1, far_index & 1, lax.axis_index("zp"), lax.axis_index("y")]).astype(jnp.int32)
    shape = jax.ShapeDtypeStruct
    f32, b16 = jnp.float32, jnp.bfloat16

    wide = far * rows
    core = lax.axis_index("c")
    cut = shape((rows // 2, anchor.shape[1]), b16)
    tiles, scaled, factor, mine, theirs = kernel_call(
        lambda *refs: prepare(far, near, rows, *refs),
        [shape((near, tokens, wide), b16), shape(key_grad.shape, b16), shape((tokens, 1), f32), cut, cut],
        (jnp.stack([fragment[0], core]).astype(jnp.int32), hidden_in, key_grad, weight_now),
        scalars=1,
    )
    other = flip(scaled, "zp", name="cotangent_pair")
    anywhere = pl.BlockSpec(memory_space=pl.ANY)
    both, tiles = pl.pallas_call(
        join_pair,
        out_shape=[shape((2 * tokens, key_width), b16), shape(tiles.shape, b16)],
        in_specs=[VMEM, VMEM, anywhere],
        out_specs=[VMEM, anywhere],
        input_output_aliases={2: 1},
        compiler_params=PARAMS,
    )(scaled, other, tiles)
    tiles = exchange(tiles, NEAR).reshape(near * tokens, wide)
    with jax.named_scope("cotangent_y"):
        turned = [lax.ppermute(both, "y", [(i, (i + k) % 4) for i in range(4)]) for k in (1, 2, 3)]

    frag_width = anchor.shape[1]
    col_offset = fragment[0] * frag_width
    part = add(mine, flip(theirs, "c"))

    part = add(part, flip(part, "x", 1))
    part = add(part, flip(part, "x", 2))

    own_gain = lax.dynamic_slice_in_dim(gain, lax.axis_index(FSDP) * rows, rows, 0)[:, None]
    weight_low = (weight_now * own_gain).astype(b16)
    near_low = swap(weight_low, 1, "weights_near")
    far_low = swap(weight_low, 2, "weights_far")
    (relayed,) = kernel_call(copy, [shape(far_low.shape, b16)], (far_low,), RELAY_COST)
    last_low = swap(relayed, 1, "weights_last")

    flops = 2 * near * tokens * far * rows * key_width
    half = key_width // 2
    block = (2, rows, half)
    keep_a, keep_b, send_a, send_b, part = kernel_call(
        lambda *refs: gradient_blocks(rows, *refs),
        [*(shape(block, f32),) * 2, *(shape(block, b16),) * 2, shape(part.shape, b16)],
        (place, part),
        flops,
        1,
        [
            pltpu.VMEM((near * tokens, key_width), b16),
            pltpu.VMEM((near * tokens, far * rows), b16),
            pltpu.SemaphoreType.DMA((12,)),
        ],
        behind=(tiles, both, *turned, near_low, last_low),
        read=5,
    )
    got_a, got_b = swap(send_a, 1, "gradient_near"), swap(send_b, 2, "gradient_far")
    (partial_keys,) = kernel_call(
        lambda *refs: key_partials(rows, multiplier, *refs),
        [shape((near // 2, 2 * tokens, key_width), b16)],
        (place, tiles, weight_low, near_low, far_low, last_low),
        KEYS_COST,
        1,
        behind=(send_a,),
    )
    mine, rest_a, rest_b = kernel_call(
        first_sum,
        [shape((rows, key_width), f32), shape((rows, half), b16), shape((rows, half), b16)],
        (keep_a, got_a, keep_b, got_b),
        FIRST_COST,
        behind=(partial_keys,),
    )
    last_a, last_b = swap(rest_a, 2, "gradient_far"), swap(rest_b, 1, "gradient_near")
    part = add(part, flip(part, "zh", name="rep_far"))
    other = flip(part, "c", name="rep_back")
    summed_cols = jnp.where(core == 0, jnp.concatenate([part, other]), jnp.concatenate([other, part])).astype(f32)
    partial_keys = exchange(partial_keys, "y")
    own_keys, pair_keys = kernel_call(
        key_halves,
        [shape((tokens, key_width), f32), shape((tokens, key_width), b16)],
        (place, partial_keys),
        scalars=1,
    )
    pair_keys = flip(pair_keys, "zp", name="keys_pair")
    (grad_sum,) = kernel_call(
        second_sum, [shape((rows, key_width), f32)], (mine, last_a, last_b), LAST_COST, behind=(own_keys,)
    )
    gradient = grad_sum * (multiplier * own_gain)
    moment_next = 0.9 * first_moment[0] + 0.1 * gradient
    second_next = 0.95 * second_moment[0].astype(f32) + 0.05 * gradient * gradient
    inner = weight_now - INNER_RATE * (
        moment_next / (jnp.sqrt(second_next) + ADAM_EPS) + 0.1 * weight_now
    )
    (keys,) = kernel_call(key_sum, [shape((tokens, key_width), b16)], (own_keys, pair_keys, factor))

    replicas = lax.axis_size(REP)
    fresh, momentum_out = outer_step(summed_cols / replicas, anchor, momentum)
    current = lax.dynamic_slice_in_dim(inner, col_offset, frag_width, 1)
    merged = 0.5 * current + 0.5 * fresh
    weights_out = lax.dynamic_update_slice_in_dim(inner, merged, col_offset, 1)
    return (keys, weights_out[None], momentum_out)


def solution(mesh):
    fine = Mesh(mesh.devices.reshape(2, 4, 2, 4, 2, 4), REP + FSDP)
    both = REP + FSDP
    return jax.shard_map(
        on_device,
        mesh=fine,
        in_specs=(
            P(both, None),
            P(),
            P(both, None),
            P(REP, FSDP, None),
            P(REP, FSDP, None),
            P(REP, FSDP, None),
            P(FSDP, None),
            P(FSDP, None),
            P(),
        ),
        out_specs=(P(both, None), P(REP, FSDP, None), P(FSDP, None)),
        check_vma=False,
    )
```
